32 devices in a mesh: parts: 2 (over y), blk: 8 (over z, x), sub: 2 (over core).
Axes of the slice: x: 2, y: 2, z: 4, core: 2. Of those that a mesh axis runs over, the one named last changes fastest.
Arguments:
- embeddings: bfloat16 [24576, 1024], P(('parts', 'blk', 'sub')), parts along dimension 0, may hold values from -6 to 6
- labels: int32 [24576], P(('parts', 'blk', 'sub')), parts along dimension 0, may hold values from 0 to 127, as said below
Outputs:
- dedup_weight: float32 [24576], P(('parts', 'blk', 'sub')), parts along dimension 0
- cluster_mass: float32 [256], P('parts'), parts along dimension 0
The draws below stay inside these ranges and needn't reach their ends.
There are 2 independent parts, one for each index of `parts`. The reference program is written for one: setup_inputs(seed, part) draws one part's arguments, and reference() takes and returns one part's arrays. A program takes and returns all parts, laid end to end along the dimension named above; each array names one. Nothing has to cross between parts.
Inputs may be any that keep to these rules, and one draw needn't show every extreme that they name: `labels`: every label of 0 to 127 occurs.
All inputs are finite; a program needn't handle non-finite values.
Results may differ from the reference program's by a relative error of at most 0.0003.
Values may be sent and summed in bfloat16 or wider, within the bound.
A program may use at most 64 MiB of HBM per device.

```python
import math
import jax
import jax.numpy as jnp
from jax import lax

D = 1024
CLUSTERS = 128
ROUNDS = 3
BLOCK = 1536
ROWS = 12288


def common_groups(key):
    group = BLOCK * (ROUNDS + 1)
    fam_per = max(1, group // 8)
    group_count = (ROWS + group - 1) // group
    family_count = group_count * fam_per
    positions = jnp.arange(ROWS, dtype=jnp.int32)
    family_rows = positions // group * fam_per + jax.random.randint(jax.random.fold_in(key, 21), (ROWS,), 0, fam_per)
    home_label = jax.random.randint(jax.random.fold_in(key, 22), (family_count,), 0, CLUSTERS)
    stray_label = jax.random.randint(jax.random.fold_in(key, 23), (ROWS,), 0, CLUSTERS)
    keeper = jax.random.randint(jax.random.fold_in(key, 24), (ROWS,), 0, 5) < 3
    label_rows = jnp.where(keeper, home_label[family_rows], stray_label)
    chosen = jax.random.permutation(jax.random.fold_in(key, 25), ROWS)[:CLUSTERS]
    label_rows = label_rows.at[chosen].set(jnp.arange(CLUSTERS, dtype=jnp.int32))
    return (label_rows.astype(jnp.int32), family_rows.astype(jnp.int32), family_count)


def draw_labels(key, part):
    label_rows, family_rows, family_count = common_groups(key)
    return label_rows


def draw_embeddings(key, part):
    label_rows, family_rows, family_count = common_groups(key)
    centers = jax.random.normal(jax.random.fold_in(key, 13), (CLUSTERS, D), jnp.float32)
    family_centers = jax.random.normal(jax.random.fold_in(key, 16), (family_count, D), jnp.float32)
    jitter = jax.random.normal(jax.random.fold_in(key, 14), (ROWS, D), jnp.float32)
    spread = jnp.exp(jax.random.uniform(jax.random.fold_in(key, 17), (ROWS,), jnp.float32, math.log(0.1), math.log(0.6)))
    values = 0.387 * centers[label_rows] + 0.922 * family_centers[family_rows] + spread[:, None] * jitter
    length = jnp.sqrt(jnp.sum(values * values, axis=1, keepdims=True))
    values = values * (math.sqrt(D) / length)
    return jnp.clip(values, -6.0, 6.0).astype(jnp.bfloat16)


def setup_inputs(seed: int = 0, part: int = 0) -> dict:
    key_of = jax.random.split(jax.random.key(seed), 3)
    own_keys = jax.random.split(jax.random.fold_in(key_of[2], part), 3)
    embeddings = draw_embeddings(jax.random.fold_in(jax.random.fold_in(key_of[2], part), 71), part)
    labels = draw_labels(jax.random.fold_in(jax.random.fold_in(key_of[2], part), 71), part)
    return {"embeddings": embeddings, "labels": labels}


TAU = 25.0


def kernel_rows(rows, row_lab, cols, col_lab):
    score = jnp.dot(rows, cols.T, preferred_element_type=jnp.float32) / D
    value = jnp.exp(TAU * (score - 1.0))
    value = jnp.where(row_lab[:, None] == col_lab[None, :], value, jnp.zeros_like(value))
    return jnp.sum(value, axis=1)


def reference(embeddings, labels):
    blocks = ROWS // BLOCK
    grouped = embeddings.reshape(blocks, BLOCK, D)
    grouped_lab = labels.reshape(blocks, BLOCK)

    def one_block(index):
        rows = grouped[index]
        row_lab = grouped_lab[index]
        total = kernel_rows(rows, row_lab, rows, row_lab)
        for mask in range(1, ROUNDS + 1):
            other = jnp.bitwise_xor(index, mask)
            total = total + kernel_rows(rows, row_lab, grouped[other], grouped_lab[other])
        return total

    density = lax.map(one_block, jnp.arange(blocks, dtype=jnp.int32))
    weight = 1.0 / density.reshape(ROWS)
    ident = jnp.arange(CLUSTERS, dtype=jnp.int32)
    mass = jnp.sum(jnp.where(labels[:, None] == ident[None, :], weight[:, None], jnp.zeros_like(weight)[:, None]), axis=0)
    return weight, mass
```

```python
import functools
import math

import jax
import jax.numpy as jnp
from jax import lax
from jax.experimental import pallas as pl
from jax.experimental.pallas import tpu as pltpu
from jax.sharding import PartitionSpec as P

CLUSTERS = 128
GROUP = 4
TAU = 25.0
MESH = pl.DeviceIdType.MESH
CHUNK = 256


def ring_swap(v):
    return v + lax.div(v, 2) - 2 * lax.div(v, 3)


def kernel(emb, lab, out_w, out_m, other, near, far, cross, labs, cols,
           near_sum, far_sum, cross_sum, send_buf, back,
           near_send, near_recv, far_send, far_recv, other_sem, cross_send,
           cross_recv, lab_send, lab_recv, back_send, back_recv):
    count, width = emb.shape
    n = count // CHUNK
    scale = TAU * math.log2(math.e) / width
    part = lax.axis_index("parts")
    blk = lax.axis_index("blk")
    core = lax.axis_index("sub")
    low = lax.rem(blk, GROUP)
    base = blk - low
    place = ring_swap(low)
    step = 1 - 2 * core

    def device(offset, c):
        return (part, base + ring_swap(lax.rem(place + offset + 2 * GROUP, GROUP)), c)

    me = place * 2 + core
    nxt = device(step, core)
    prv = device(-step, core)
    sib = device(0, 1 - core)
    opp = device(2, core)
    skew = device(step, 1 - core)

    def who(offset, c):
        return lax.rem(place + offset + 2 * GROUP, GROUP) * 2 + c

    barrier = pltpu.get_barrier_semaphore()
    others = [(o, x) for o in range(GROUP) for x in range(2) if (o, x) != (0, 0)]
    for o, x in others:
        pl.semaphore_signal(barrier, inc=1, device_id=device(o, x + core - 2 * x * core),
                            device_id_type=MESH)
    pl.semaphore_wait(barrier, len(others))

    def rows(c):
        return pl.ds(pl.multiple_of(c * CHUNK, CHUNK), CHUNK)

    def copy(src, dst, s, r, dev):
        return pltpu.make_async_remote_copy(src_ref=src, dst_ref=dst, send_sem=s, recv_sem=r,
                                            device_id=dev, device_id_type=MESH)

    def near_copy(c):
        return copy(emb.at[rows(c)], near.at[rows(c)], near_send.at[c], near_recv.at[c], nxt)

    def far_copy(c):
        return copy(near.at[rows(c)], far.at[rows(c)], far_send.at[c], far_recv.at[c], nxt)

    def cross_copy(c):
        return copy(near.at[rows(c)], cross.at[rows(c)], cross_send.at[c], cross_recv.at[c], sib)

    def other_copy():
        return copy(emb, other, other_sem.at[0], other_sem.at[1], sib)

    def lab_copy(k):
        o, x = others[k]
        c = x + core - 2 * x * core
        sent = copy(lab, labs.at[me], lab_send.at[k], lab_recv.at[me], device(o, c))
        src = who(o, c)
        got = copy(lab, labs.at[src], lab_send.at[k], lab_recv.at[src], device(o, c))
        return sent, got

    for k in range(len(others)):
        lab_copy(k)[0].start()

    @pl.loop(0, n)
    def _(c):
        near_copy(c).start()

    other_copy().start()

    def column(row):
        return jnp.broadcast_to(row, (128, count)).T

    own_lab = lab[...]
    cols[0] = column(own_lab)

    def tile(x, xlab, y, ylab):
        s = lax.dot_general(x, y, (((1,), (1,)), ((), ())), preferred_element_type=jnp.float32)
        v = jnp.exp2((s - float(width)) * scale)
        same = jnp.concatenate([xlab] * (count // 128), axis=1) == ylab
        return jnp.where(same, v, 0.0)

    def colsum(v):
        return jnp.sum(v, axis=0, keepdims=True)

    def rowpart(v):
        t = v[:, :128]
        for k in range(1, count // 128):
            t = t + v[:, k * 128:(k + 1) * 128]
        return t

    def own_tile(ref, slot, c):
        return tile(ref[rows(c), :], cols[slot, rows(c), :], emb[...], own_lab)

    zero = jnp.zeros((1, count), jnp.float32)
    own = lax.fori_loop(0, n, lambda c, a: a + colsum(own_tile(emb, 0, c)), zero)

    for k in range(len(others)):
        sent, got = lab_copy(k)
        got.wait_recv()
    cols[1] = column(labs[who(0, 1 - core)])
    cols[2] = column(labs[who(-step, core)])
    cols[3] = column(labs[who(step, 1 - core)])
    cols[4] = column(labs[who(2, core)])
    cross_lab = labs[who(step, 1 - core)]

    other_copy().wait_recv()
    own = lax.fori_loop(0, n, lambda c, a: a + colsum(own_tile(other, 1, c)), own)

    def near_step(c, a):
        near_copy(c).wait_recv()
        far_copy(c).start()
        cross_copy(c).start()
        v = own_tile(near, 2, c)
        near_sum[rows(c), :] = rowpart(v)
        return a + colsum(v)

    own = lax.fori_loop(0, n, near_step, own)

    def cross_step(c, a):
        cross_copy(c).wait_recv()
        return a + colsum(own_tile(cross, 3, c))

    own = lax.fori_loop(0, n, cross_step, own)
    cross_sum[...] = zero

    @pl.when(core == 1)
    def _():
        @pl.loop(0, n)
        def _(c):
            v = tile(near[rows(c), :], cols[2, rows(c), :], cross[...], cross_lab)
            near_sum[rows(c), :] += rowpart(v)
            cross_sum[...] += colsum(v)

    def back_copy(k, dev):
        return copy(send_buf.at[k], back.at[k], back_send.at[k], back_recv.at[k], dev)

    send_buf[0] = colsum(near_sum[...].T)
    back_copy(0, prv).start()

    def far_step(c, a):
        far_copy(c).wait_recv()

        @pl.when(core == 0)
        def _():
            v = tile(far[rows(c), :], cols[4, rows(c), :], cross[...], cross_lab)
            far_sum[rows(c), :] = rowpart(v)
            cross_sum[...] += colsum(v)

            @pl.when(c == n - 1)
            def _():
                send_buf[1] = colsum(far_sum[...].T)
                send_buf[2] = cross_sum[...]
                back_copy(1, opp).start()
                back_copy(2, skew).start()

        @pl.when((core == 1) & (c == 0))
        def _():
            send_buf[1] = zero
            send_buf[2] = cross_sum[...]
            back_copy(1, opp).start()
            back_copy(2, skew).start()

        return a + colsum(own_tile(far, 4, c))

    own = lax.fori_loop(0, n, far_step, own)

    for k, dev in enumerate((prv, opp, skew)):
        back_copy(k, dev).wait_recv()
        own = own + back[k]

    weight = 1.0 / own
    out_w[...] = weight
    ident = lax.broadcasted_iota(jnp.int32, (CLUSTERS, count), 0)
    out_m[...] = colsum(rowpart(jnp.where(ident == own_lab, weight, 0.0)).T)

    @pl.loop(0, n)
    def _(c):
        near_copy(c).wait_send()
        far_copy(c).wait_send()
        cross_copy(c).wait_send()

    other_copy().wait_send()
    for k in range(len(others)):
        lab_copy(k)[0].wait_send()
    for k, dev in enumerate((prv, opp, skew)):
        back_copy(k, dev).wait_send()


def per_device(embeddings, labels):
    count, width = embeddings.shape
    n = count // CHUNK
    f32, i32, bf16 = jnp.float32, jnp.int32, jnp.bfloat16
    dma = pltpu.SemaphoreType.DMA
    vmem = pl.BlockSpec(memory_space=pltpu.VMEM)
    weight, mass = pl.pallas_call(
        kernel,
        out_shape=(jax.ShapeDtypeStruct((1, count), f32), jax.ShapeDtypeStruct((1, CLUSTERS), f32)),
        in_specs=[vmem, vmem],
        out_specs=(vmem, vmem),
        scratch_shapes=[
            pltpu.VMEM((count, width), bf16),
            pltpu.VMEM((count, width), bf16),
            pltpu.VMEM((count, width), bf16),
            pltpu.VMEM((count, width), bf16),
            pltpu.VMEM((2 * GROUP, 1, count), i32),
            pltpu.VMEM((5, count, 128), i32),
            pltpu.VMEM((count, 128), f32),
            pltpu.VMEM((count, 128), f32),
            pltpu.VMEM((1, count), f32),
            pltpu.VMEM((3, 1, count), f32),
            pltpu.VMEM((3, 1, count), f32),
            dma((n,)), dma((n,)), dma((n,)), dma((n,)), dma((2,)), dma((n,)), dma((n,)),
            dma((2 * GROUP - 1,)), dma((2 * GROUP,)), dma((3,)), dma((3,)),
        ],
        compiler_params=pltpu.CompilerParams(
            collective_id=0, has_side_effects=True, vmem_limit_bytes=48 * 1024 * 1024),
        cost_estimate=pl.CostEstimate(flops=12 * count * count * width, bytes_accessed=2 * count * width,
                                      transcendentals=6 * count * count),
    )(embeddings, labels.reshape(1, count))
    return weight.reshape(count), lax.psum(mass.reshape(CLUSTERS), ("blk", "sub"))


def solution(mesh):
    in_specs = (P(("parts", "blk", "sub"), None), P(("parts", "blk", "sub")))
    out_specs = (P(("parts", "blk", "sub")), P("parts"))
    return jax.shard_map(
        per_device, mesh=mesh, in_specs=in_specs, out_specs=out_specs, check_vma=False
    )
```

```python
import functools
import math

import jax
import jax.numpy as jnp
from jax import lax
from jax.experimental import pallas as pl
from jax.experimental.pallas import tpu as pltpu
from jax.sharding import PartitionSpec as P

CLUSTERS = 128
GROUP = 4
TAU = 25.0
MESH = pl.DeviceIdType.MESH
CHUNK = 256


def ring_swap(v):
    return v + lax.div(v, 2) - 2 * lax.div(v, 3)


def kernel(src, lab1, out_w, out_m, emb, lab, masses, other, near, far, cross, labs, cols,
           near_sum, far_sum, cross_sum, send_buf, back,
           near_send, near_recv, far_send, far_recv, other_sem, cross_send,
           cross_recv, lab_send, lab_recv, back_send, back_recv,
           local_sem, mass_send, mass_recv):
    count, width = emb.shape
    n = count // CHUNK
    scale = TAU * math.log2(math.e) / width
    part = lax.axis_index("parts")
    blk = lax.axis_index("blk")
    core = lax.axis_index("sub")
    low = lax.rem(blk, GROUP)
    base = blk - low
    place = ring_swap(low)
    step = 1 - 2 * core
    total = 2 * lax.axis_size("blk")
    index = 2 * blk + core
    load = pltpu.make_async_copy(src, emb, local_sem.at[0])
    load.start()
    lab[...] = lab1[...].reshape(1, count)

    def device(offset, c):
        return (part, base + ring_swap(lax.rem(place + offset + 2 * GROUP, GROUP)), c)

    me = place * 2 + core
    nxt = device(step, core)
    prv = device(-step, core)
    sib = device(0, 1 - core)
    opp = device(2, core)
    skew = device(step, 1 - core)

    def who(offset, c):
        return lax.rem(place + offset + 2 * GROUP, GROUP) * 2 + c

    others = [(o, x) for o in range(GROUP) for x in range(2) if (o, x) != (0, 0)]

    def member(k):
        t = lax.rem(index + k, total)
        return t, (part, lax.div(t, 2), lax.rem(t, 2))

    barrier = pltpu.get_barrier_semaphore()

    @pl.loop(1, total)
    def _(k):
        pl.semaphore_signal(barrier, inc=1, device_id=member(k)[1], device_id_type=MESH)

    pl.semaphore_wait(barrier, total - 1)

    def rows(c):
        return pl.ds(pl.multiple_of(c * CHUNK, CHUNK), CHUNK)

    def copy(src, dst, s, r, dev):
        return pltpu.make_async_remote_copy(src_ref=src, dst_ref=dst, send_sem=s, recv_sem=r,
                                            device_id=dev, device_id_type=MESH)

    def near_copy(c):
        return copy(src.at[rows(c)], near.at[rows(c)], near_send.at[c], near_recv.at[c], nxt)

    def far_copy(c):
        return copy(near.at[rows(c)], far.at[rows(c)], far_send.at[c], far_recv.at[c], nxt)

    def cross_copy(c):
        return copy(near.at[rows(c)], cross.at[rows(c)], cross_send.at[c], cross_recv.at[c], sib)

    def other_copy():
        return copy(src, other, other_sem.at[0], other_sem.at[1], sib)

    def lab_copy(k):
        o, x = others[k]
        c = x + core - 2 * x * core
        sent = copy(lab, labs.at[me], lab_send.at[k], lab_recv.at[me], device(o, c))
        src = who(o, c)
        got = copy(lab, labs.at[src], lab_send.at[k], lab_recv.at[src], device(o, c))
        return sent, got

    @pl.loop(0, n)
    def _(c):
        near_copy(c).start()

    for k in range(len(others)):
        lab_copy(k)[0].start()
    other_copy().start()

    def column(row):
        return jnp.broadcast_to(row, (128, count)).T

    own_lab = lab[...]
    cols[0] = column(own_lab)
    load.wait()

    def tile(x, xlab, y, ylab):
        s = lax.dot_general(x, y, (((1,), (1,)), ((), ())), preferred_element_type=jnp.float32)
        v = jnp.exp2((s - float(width)) * scale)
        same = jnp.concatenate([xlab] * (count // 128), axis=1) == ylab
        return jnp.where(same, v, 0.0)

    def colsum(v):
        return jnp.sum(v, axis=0, keepdims=True)

    def rowpart(v):
        t = v[:, :128]
        for k in range(1, count // 128):
            t = t + v[:, k * 128:(k + 1) * 128]
        return t

    def own_tile(ref, slot, c):
        return tile(ref[rows(c), :], cols[slot, rows(c), :], emb[...], own_lab)

    zero = jnp.zeros((1, count), jnp.float32)
    own = lax.fori_loop(0, n, lambda c, a: a + colsum(own_tile(emb, 0, c)), zero)

    for k in range(len(others)):
        sent, got = lab_copy(k)
        got.wait_recv()
    cols[1] = column(labs[who(0, 1 - core)])
    cols[2] = column(labs[who(-step, core)])
    cols[3] = column(labs[who(step, 1 - core)])
    cols[4] = column(labs[who(2, core)])
    cross_lab = labs[who(step, 1 - core)]

    other_copy().wait_recv()
    own = lax.fori_loop(0, n, lambda c, a: a + colsum(own_tile(other, 1, c)), own)

    def near_step(c, a):
        near_copy(c).wait_recv()
        far_copy(c).start()
        cross_copy(c).start()
        v = own_tile(near, 2, c)
        near_sum[rows(c), :] = rowpart(v)
        return a + colsum(v)

    own = lax.fori_loop(0, n, near_step, own)

    def cross_step(c, a):
        cross_copy(c).wait_recv()
        return a + colsum(own_tile(cross, 3, c))

    own = lax.fori_loop(0, n, cross_step, own)
    cross_sum[...] = zero

    @pl.when(core == 1)
    def _():
        @pl.loop(0, n)
        def _(c):
            v = tile(near[rows(c), :], cols[2, rows(c), :], cross[...], cross_lab)
            near_sum[rows(c), :] += rowpart(v)
            cross_sum[...] += colsum(v)

    def back_copy(k, dev):
        return copy(send_buf.at[k], back.at[k], back_send.at[k], back_recv.at[k], dev)

    send_buf[0] = colsum(near_sum[...].T)
    back_copy(0, prv).start()

    def far_step(c, a):
        far_copy(c).wait_recv()

        @pl.when(core == 0)
        def _():
            v = tile(far[rows(c), :], cols[4, rows(c), :], cross[...], cross_lab)
            far_sum[rows(c), :] = rowpart(v)
            cross_sum[...] += colsum(v)

            @pl.when(c == n - 1)
            def _():
                send_buf[1] = colsum(far_sum[...].T)
                send_buf[2] = cross_sum[...]
                back_copy(1, opp).start()
                back_copy(2, skew).start()

        @pl.when((core == 1) & (c == 0))
        def _():
            send_buf[1] = zero
            send_buf[2] = cross_sum[...]
            back_copy(1, opp).start()
            back_copy(2, skew).start()

        return a + colsum(own_tile(far, 4, c))

    own = lax.fori_loop(0, n, far_step, own)

    for k, dev in enumerate((prv, opp, skew)):
        back_copy(k, dev).wait_recv()
        own = own + back[k]

    weight = 1.0 / own
    ident = lax.broadcasted_iota(jnp.int32, (CLUSTERS, count), 0)
    masses[index] = colsum(rowpart(jnp.where(ident == own_lab, weight, 0.0)).T)

    def mass_copy(k):
        t, dev = member(k)
        sent = copy(masses.at[index], masses.at[index], mass_send.at[k], mass_recv.at[index], dev)
        got = copy(masses.at[t], masses.at[t], mass_send.at[k], mass_recv.at[t], dev)
        return sent, got

    @pl.loop(1, total)
    def _(k):
        mass_copy(k)[0].start()

    out_w[...] = weight.reshape(count)

    @pl.loop(0, n)
    def _(c):
        near_copy(c).wait_send()
        far_copy(c).wait_send()
        cross_copy(c).wait_send()

    other_copy().wait_send()
    for k in range(len(others)):
        lab_copy(k)[0].wait_send()
    for k, dev in enumerate((prv, opp, skew)):
        back_copy(k, dev).wait_send()

    @pl.loop(1, total)
    def _(k):
        mass_copy(k)[1].wait_recv()

    out_m[...] = jnp.sum(masses[...], axis=0).reshape(CLUSTERS)

    @pl.loop(1, total)
    def _(k):
        mass_copy(k)[0].wait_send()


def per_device(embeddings, labels):
    count, width = embeddings.shape
    n = count // CHUNK
    total = 2 * lax.axis_size("blk")
    f32, i32, bf16 = jnp.float32, jnp.int32, jnp.bfloat16
    dma = pltpu.SemaphoreType.DMA
    vmem = pl.BlockSpec(memory_space=pltpu.VMEM)
    weight, mass = pl.pallas_call(
        kernel,
        out_shape=(jax.ShapeDtypeStruct((count,), f32), jax.ShapeDtypeStruct((CLUSTERS,), f32)),
        in_specs=[pl.BlockSpec(memory_space=pltpu.HBM), vmem],
        out_specs=(vmem, vmem),
        scratch_shapes=[
            pltpu.VMEM((count, width), bf16),
            pltpu.VMEM((1, count), i32),
            pltpu.VMEM((total, 1, CLUSTERS), f32),
            pltpu.VMEM((count, width), bf16),
            pltpu.VMEM((count, width), bf16),
            pltpu.VMEM((count, width), bf16),
            pltpu.VMEM((count, width), bf16),
            pltpu.VMEM((2 * GROUP, 1, count), i32),
            pltpu.VMEM((5, count, 128), i32),
            pltpu.VMEM((count, 128), f32),
            pltpu.VMEM((count, 128), f32),
            pltpu.VMEM((1, count), f32),
            pltpu.VMEM((3, 1, count), f32),
            pltpu.VMEM((3, 1, count), f32),
            dma((n,)), dma((n,)), dma((n,)), dma((n,)), dma((2,)), dma((n,)), dma((n,)),
            dma((2 * GROUP - 1,)), dma((2 * GROUP,)), dma((3,)), dma((3,)),
            dma((1,)), dma((total,)), dma((total,)),
        ],
        compiler_params=pltpu.CompilerParams(
            collective_id=0, has_side_effects=True, vmem_limit_bytes=48 * 1024 * 1024),
        cost_estimate=pl.CostEstimate(flops=12 * count * count * width, bytes_accessed=2 * count * width,
                                      transcendentals=6 * count * count),
    )(embeddings, labels)
    return weight, mass


def solution(mesh):
    in_specs = (P(("parts", "blk", "sub"), None), P(("parts", "blk", "sub")))
    out_specs = (P(("parts", "blk", "sub")), P("parts"))
    return jax.shard_map(
        per_device, mesh=mesh, in_specs=in_specs, out_specs=out_specs, check_vma=False
    )
```

```python
import functools
import math

import jax
import jax.numpy as jnp
from jax import lax
from jax.experimental import pallas as pl
from jax.experimental.pallas import tpu as pltpu
from jax.sharding import PartitionSpec as P

CLUSTERS = 128
GROUP = 4
TAU = 25.0
MESH = pl.DeviceIdType.MESH
CHUNK = 256


def ring_swap(v):
    return v + lax.div(v, 2) - 2 * lax.div(v, 3)


def kernel(src, lab1, out_w, out_m, emb, lab, masses, other, near, far, cross, labs, cols,
           near_sum, far_sum, cross_sum, send_buf, back,
           near_send, near_recv, far_send, far_recv, other_sem, cross_send,
           cross_recv, lab_send, lab_recv, back_send, back_recv,
           local_sem, mass_send, mass_recv):
    count, width = emb.shape
    n = count // CHUNK
    scale = TAU * math.log2(math.e) / width
    part = lax.axis_index("parts")
    blk = lax.axis_index("blk")
    core = lax.axis_index("sub")
    low = lax.rem(blk, GROUP)
    base = blk - low
    place = ring_swap(low)
    step = 1 - 2 * core
    total = 2 * lax.axis_size("blk")
    index = 2 * blk + core
    load = pltpu.make_async_copy(src, emb, local_sem.at[0])
    load.start()
    lab[...] = lab1[...].reshape(1, count)

    def device(offset, c):
        return (part, base + ring_swap(lax.rem(place + offset + 2 * GROUP, GROUP)), c)

    me = place * 2 + core
    nxt = device(step, core)
    prv = device(-step, core)
    sib = device(0, 1 - core)
    opp = device(2, core)
    skew = device(step, 1 - core)

    def who(offset, c):
        return lax.rem(place + offset + 2 * GROUP, GROUP) * 2 + c

    others = [(o, x) for o in range(GROUP) for x in range(2) if (o, x) != (0, 0)]

    def member(k):
        t = lax.rem(index + k, total)
        return t, (part, lax.div(t, 2), lax.rem(t, 2))

    barrier = pltpu.get_barrier_semaphore()

    @pl.loop(1, total)
    def _(k):
        pl.semaphore_signal(barrier, inc=1, device_id=member(k)[1], device_id_type=MESH)

    pl.semaphore_wait(barrier, total - 1)

    def rows(c):
        return pl.ds(pl.multiple_of(c * CHUNK, CHUNK), CHUNK)

    def copy(src, dst, s, r, dev):
        return pltpu.make_async_remote_copy(src_ref=src, dst_ref=dst, send_sem=s, recv_sem=r,
                                            device_id=dev, device_id_type=MESH)

    def near_copy(c):
        return copy(src.at[rows(c)], near.at[rows(c)], near_send.at[c], near_recv.at[c], nxt)

    def far_copy(c):
        return copy(near.at[rows(c)], far.at[rows(c)], far_send.at[c], far_recv.at[c], nxt)

    def cross_copy(c):
        return copy(near.at[rows(c)], cross.at[rows(c)], cross_send.at[c], cross_recv.at[c], sib)

    def other_copy():
        return copy(src, other, other_sem.at[0], other_sem.at[1], sib)

    def lab_copy(k):
        o, x = others[k]
        c = x + core - 2 * x * core
        sent = copy(lab, labs.at[me], lab_send.at[k], lab_recv.at[me], device(o, c))
        src = who(o, c)
        got = copy(lab, labs.at[src], lab_send.at[k], lab_recv.at[src], device(o, c))
        return sent, got

    for k in range(len(others)):
        lab_copy(k)[0].start()

    @pl.loop(0, n)
    def _(c):
        near_copy(c).start()

    other_copy().start()

    def column(row):
        return jnp.broadcast_to(row, (128, count)).T

    own_lab = lab[...]
    cols[0] = column(own_lab)
    load.wait()

    def tile(x, xlab, y, ylab):
        s = lax.dot_general(x, y, (((1,), (1,)), ((), ())), preferred_element_type=jnp.float32)
        v = jnp.exp2((s - float(width)) * scale)
        same = jnp.concatenate([xlab] * (count // 128), axis=1) == ylab
        return jnp.where(same, v, 0.0)

    def colsum(v):
        return jnp.sum(v, axis=0, keepdims=True)

    def rowpart(v):
        t = v[:, :128]
        for k in range(1, count // 128):
            t = t + v[:, k * 128:(k + 1) * 128]
        return t

    def own_tile(ref, slot, c):
        return tile(ref[rows(c), :], cols[slot, rows(c), :], emb[...], own_lab)

    zero = jnp.zeros((1, count), jnp.float32)
    own = lax.fori_loop(0, n, lambda c, a: a + colsum(own_tile(emb, 0, c)), zero)

    for k in range(len(others)):
        sent, got = lab_copy(k)
        got.wait_recv()
    cols[1] = column(labs[who(0, 1 - core)])
    cols[2] = column(labs[who(-step, core)])
    cols[3] = column(labs[who(step, 1 - core)])
    cols[4] = column(labs[who(2, core)])
    cross_lab = labs[who(step, 1 - core)]

    def near_step(c, a):
        near_copy(c).wait_recv()
        far_copy(c).start()
        cross_copy(c).start()
        v = own_tile(near, 2, c)
        near_sum[rows(c), :] = rowpart(v)
        return a + colsum(v)

    own = lax.fori_loop(0, n, near_step, own)

    other_copy().wait_recv()
    own = lax.fori_loop(0, n, lambda c, a: a + colsum(own_tile(other, 1, c)), own)

    def cross_step(c, a):
        cross_copy(c).wait_recv()
        return a + colsum(own_tile(cross, 3, c))

    own = lax.fori_loop(0, n, cross_step, own)
    cross_sum[...] = zero

    @pl.when(core == 1)
    def _():
        @pl.loop(0, n)
        def _(c):
            v = tile(near[rows(c), :], cols[2, rows(c), :], cross[...], cross_lab)
            near_sum[rows(c), :] += rowpart(v)
            cross_sum[...] += colsum(v)

    def back_copy(k, dev):
        return copy(send_buf.at[k], back.at[k], back_send.at[k], back_recv.at[k], dev)

    send_buf[0] = colsum(near_sum[...].T)
    back_copy(0, prv).start()

    def far_step(c, a):
        far_copy(c).wait_recv()

        @pl.when(core == 0)
        def _():
            v = tile(far[rows(c), :], cols[4, rows(c), :], cross[...], cross_lab)
            far_sum[rows(c), :] = rowpart(v)
            cross_sum[...] += colsum(v)

            @pl.when(c == n - 1)
            def _():
                send_buf[1] = colsum(far_sum[...].T)
                send_buf[2] = cross_sum[...]
                back_copy(1, opp).start()
                back_copy(2, skew).start()

        @pl.when((core == 1) & (c == 0))
        def _():
            send_buf[1] = zero
            send_buf[2] = cross_sum[...]
            back_copy(1, opp).start()
            back_copy(2, skew).start()

        return a + colsum(own_tile(far, 4, c))

    own = lax.fori_loop(0, n, far_step, own)

    for k, dev in enumerate((prv, opp, skew)):
        back_copy(k, dev).wait_recv()
        own = own + back[k]

    weight = 1.0 / own
    ident = lax.broadcasted_iota(jnp.int32, (CLUSTERS, count), 0)
    masses[index] = colsum(rowpart(jnp.where(ident == own_lab, weight, 0.0)).T)

    def mass_copy(k):
        t, dev = member(k)
        sent = copy(masses.at[index], masses.at[index], mass_send.at[k], mass_recv.at[index], dev)
        got = copy(masses.at[t], masses.at[t], mass_send.at[k], mass_recv.at[t], dev)
        return sent, got

    @pl.loop(1, total)
    def _(k):
        mass_copy(k)[0].start()

    out_w[...] = weight.reshape(count)

    @pl.loop(0, n)
    def _(c):
        near_copy(c).wait_send()
        far_copy(c).wait_send()
        cross_copy(c).wait_send()

    other_copy().wait_send()
    for k in range(len(others)):
        lab_copy(k)[0].wait_send()
    for k, dev in enumerate((prv, opp, skew)):
        back_copy(k, dev).wait_send()

    @pl.loop(1, total)
    def _(k):
        mass_copy(k)[1].wait_recv()

    out_m[...] = jnp.sum(masses[...], axis=0).reshape(CLUSTERS)

    @pl.loop(1, total)
    def _(k):
        mass_copy(k)[0].wait_send()


def per_device(embeddings, labels):
    count, width = embeddings.shape
    n = count // CHUNK
    total = 2 * lax.axis_size("blk")
    f32, i32, bf16 = jnp.float32, jnp.int32, jnp.bfloat16
    dma = pltpu.SemaphoreType.DMA
    vmem = pl.BlockSpec(memory_space=pltpu.VMEM)
    weight, mass = pl.pallas_call(
        kernel,
        out_shape=(jax.ShapeDtypeStruct((count,), f32), jax.ShapeDtypeStruct((CLUSTERS,), f32)),
        in_specs=[pl.BlockSpec(memory_space=pltpu.HBM), vmem],
        out_specs=(vmem, vmem),
        scratch_shapes=[
            pltpu.VMEM((count, width), bf16),
            pltpu.VMEM((1, count), i32),
            pltpu.VMEM((total, 1, CLUSTERS), f32),
            pltpu.VMEM((count, width), bf16),
            pltpu.VMEM((count, width), bf16),
            pltpu.VMEM((count, width), bf16),
            pltpu.VMEM((count, width), bf16),
            pltpu.VMEM((2 * GROUP, 1, count), i32),
            pltpu.VMEM((5, count, 128), i32),
            pltpu.VMEM((count, 128), f32),
            pltpu.VMEM((count, 128), f32),
            pltpu.VMEM((1, count), f32),
            pltpu.VMEM((3, 1, count), f32),
            pltpu.VMEM((3, 1, count), f32),
            dma((n,)), dma((n,)), dma((n,)), dma((n,)), dma((2,)), dma((n,)), dma((n,)),
            dma((2 * GROUP - 1,)), dma((2 * GROUP,)), dma((3,)), dma((3,)),
            dma((1,)), dma((total,)), dma((total,)),
        ],
        compiler_params=pltpu.CompilerParams(
            collective_id=0, has_side_effects=True, vmem_limit_bytes=63 * 1024 * 1024),
        cost_estimate=pl.CostEstimate(flops=12 * count * count * width, bytes_accessed=2 * count * width,
                                      transcendentals=6 * count * count),
    )(embeddings, labels)
    return weight, mass


def solution(mesh):
    in_specs = (P(("parts", "blk", "sub"), None), P(("parts", "blk", "sub")))
    out_specs = (P(("parts", "blk", "sub")), P("parts"))
    return jax.shard_map(
        per_device, mesh=mesh, in_specs=in_specs, out_specs=out_specs, check_vma=False
    )
```

```python
import functools
import math

import jax
import jax.numpy as jnp
from jax import lax
from jax.experimental import pallas as pl
from jax.experimental.pallas import tpu as pltpu
from jax.sharding import PartitionSpec as P

CLUSTERS = 128
GROUP = 4
TAU = 25.0
MESH = pl.DeviceIdType.MESH
CHUNK = 256


def ring_swap(v):
    return v + lax.div(v, 2) - 2 * lax.div(v, 3)


def kernel(src, lab1, out_w, out_m, emb, flat, lab, masses, other, near, far, cross, labs, cols,
           near_sum, cross_sum, send_buf, back,
           near_send, near_recv, far_send, far_recv, other_sem, cross_send,
           cross_recv, lab_send, lab_recv, back_send, back_recv,
           local_sem, mass_send, mass_recv):
    count, width = emb.shape
    n = count // CHUNK
    scale = TAU * math.log2(math.e) / width
    part = lax.axis_index("parts")
    blk = lax.axis_index("blk")
    core = lax.axis_index("sub")
    low = lax.rem(blk, GROUP)
    base = blk - low
    place = ring_swap(low)
    step = 1 - 2 * core
    total = 2 * lax.axis_size("blk")
    index = 2 * blk + core
    load = pltpu.make_async_copy(src, emb, local_sem.at[0])
    load.start()
    load_lab = pltpu.make_async_copy(lab1, flat, local_sem.at[1])
    load_lab.start()

    def device(offset, c):
        return (part, base + ring_swap(lax.rem(place + offset + 2 * GROUP, GROUP)), c)

    me = place * 2 + core
    nxt = device(step, core)
    prv = device(-step, core)
    sib = device(0, 1 - core)
    opp = device(2, core)
    skew = device(step, 1 - core)

    def who(offset, c):
        return lax.rem(place + offset + 2 * GROUP, GROUP) * 2 + c

    others = [(o, x) for o in range(GROUP) for x in range(2) if (o, x) != (0, 0)]

    def member(k):
        t = lax.rem(index + k, total)
        return t, (part, lax.div(t, 2), lax.rem(t, 2))

    barrier = pltpu.get_barrier_semaphore()

    @pl.loop(1, total)
    def _(k):
        pl.semaphore_signal(barrier, inc=1, device_id=member(k)[1], device_id_type=MESH)

    load_lab.wait()
    lab[...] = flat[...].reshape(1, count)
    pl.semaphore_wait(barrier, total - 1)

    def rows(c):
        return pl.ds(pl.multiple_of(c * CHUNK, CHUNK), CHUNK)

    def copy(src, dst, s, r, dev):
        return pltpu.make_async_remote_copy(src_ref=src, dst_ref=dst, send_sem=s, recv_sem=r,
                                            device_id=dev, device_id_type=MESH)

    def near_copy(c):
        return copy(src.at[rows(c)], near.at[rows(c)], near_send.at[c], near_recv.at[c], nxt)

    def far_copy(c):
        return copy(near.at[rows(c)], far.at[rows(c)], far_send.at[c], far_recv.at[c], nxt)

    def cross_copy(c):
        return copy(near.at[rows(c)], cross.at[rows(c)], cross_send.at[c], cross_recv.at[c], sib)

    def other_copy():
        return copy(src, other, other_sem.at[0], other_sem.at[1], sib)

    def lab_copy(k):
        o, x = others[k]
        c = x + core - 2 * x * core
        sent = copy(lab, labs.at[me], lab_send.at[k], lab_recv.at[me], device(o, c))
        src = who(o, c)
        got = copy(lab, labs.at[src], lab_send.at[k], lab_recv.at[src], device(o, c))
        return sent, got

    for k in range(len(others)):
        lab_copy(k)[0].start()

    @pl.loop(0, n)
    def _(c):
        near_copy(c).start()

    other_copy().start()

    def column(row):
        return jnp.broadcast_to(row, (128, count)).T

    own_lab = lab[...]
    cols[0] = column(own_lab)
    load.wait()

    def tile(x, xlab, y, ylab):
        s = lax.dot_general(x, y, (((1,), (1,)), ((), ())), preferred_element_type=jnp.float32)
        v = jnp.exp2((s - float(width)) * scale)
        same = jnp.concatenate([xlab] * (count // 128), axis=1) == ylab
        return jnp.where(same, v, 0.0)

    def colsum(v):
        return jnp.sum(v, axis=0, keepdims=True)

    def rowpart(v):
        t = v[:, :128]
        for k in range(1, count // 128):
            t = t + v[:, k * 128:(k + 1) * 128]
        return t

    def own_tile(ref, slot, c):
        return tile(ref[rows(c), :], cols[slot, rows(c), :], emb[...], own_lab)

    zero = jnp.zeros((1, count), jnp.float32)
    own = lax.fori_loop(0, n, lambda c, a: a + colsum(own_tile(emb, 0, c)), zero)

    for k in range(len(others)):
        sent, got = lab_copy(k)
        got.wait_recv()
    cols[1] = column(labs[who(0, 1 - core)])
    cols[2] = column(labs[who(-step, core)])
    cols[3] = column(labs[who(step, 1 - core)])
    cols[4] = column(labs[who(2, core)])
    cross_lab = labs[who(step, 1 - core)]

    def near_step(c, a):
        near_copy(c).wait_recv()
        far_copy(c).start()
        cross_copy(c).start()
        v = own_tile(near, 2, c)
        near_sum[rows(c), :] = rowpart(v)
        return a + colsum(v)

    own = lax.fori_loop(0, n, near_step, own)

    other_copy().wait_recv()
    own = lax.fori_loop(0, n, lambda c, a: a + colsum(own_tile(other, 1, c)), own)

    def cross_step(c, a):
        cross_copy(c).wait_recv()
        return a + colsum(own_tile(cross, 3, c))

    own = lax.fori_loop(0, n, cross_step, own)
    cross_sum[...] = zero

    @pl.when(core == 1)
    def _():
        @pl.loop(0, n)
        def _(c):
            v = tile(near[rows(c), :], cols[2, rows(c), :], cross[...], cross_lab)
            near_sum[rows(c), :] += rowpart(v)
            cross_sum[...] += colsum(v)

    def back_copy(k, dev):
        return copy(send_buf.at[k], back.at[k], back_send.at[k], back_recv.at[k], dev)

    send_buf[0] = colsum(near_sum[...].T)
    back_copy(0, prv).start()

    def far_step(c, a):
        far_copy(c).wait_recv()

        @pl.when(core == 0)
        def _():
            v = tile(far[rows(c), :], cols[4, rows(c), :], cross[...], cross_lab)
            send_buf[1, :, rows(c)] = colsum(rowpart(v).T)
            cross_sum[...] += colsum(v)

            @pl.when(c == n - 1)
            def _():
                send_buf[2] = cross_sum[...]
                back_copy(1, opp).start()
                back_copy(2, skew).start()

        @pl.when((core == 1) & (c == 0))
        def _():
            send_buf[1] = zero
            send_buf[2] = cross_sum[...]
            back_copy(1, opp).start()
            back_copy(2, skew).start()

        return a + colsum(own_tile(far, 4, c))

    own = lax.fori_loop(0, n, far_step, own)

    for k, dev in enumerate((prv, opp, skew)):
        back_copy(k, dev).wait_recv()
        own = own + back[k]

    weight = 1.0 / own
    ident = lax.broadcasted_iota(jnp.int32, (CLUSTERS, count), 0)
    masses[index] = colsum(rowpart(jnp.where(ident == own_lab, weight, 0.0)).T)

    def mass_copy(k):
        t, dev = member(k)
        sent = copy(masses.at[index], masses.at[index], mass_send.at[k], mass_recv.at[index], dev)
        got = copy(masses.at[t], masses.at[t], mass_send.at[k], mass_recv.at[t], dev)
        return sent, got

    @pl.loop(1, total)
    def _(k):
        mass_copy(k)[0].start()

    out_w[...] = weight.reshape(count)

    @pl.loop(0, n)
    def _(c):
        near_copy(c).wait_send()
        far_copy(c).wait_send()
        cross_copy(c).wait_send()

    other_copy().wait_send()
    for k in range(len(others)):
        lab_copy(k)[0].wait_send()
    for k, dev in enumerate((prv, opp, skew)):
        back_copy(k, dev).wait_send()

    @pl.loop(1, total)
    def _(k):
        mass_copy(k)[1].wait_recv()

    out_m[...] = jnp.sum(masses[...], axis=0).reshape(CLUSTERS)

    @pl.loop(1, total)
    def _(k):
        mass_copy(k)[0].wait_send()


def per_device(embeddings, labels):
    count, width = embeddings.shape
    n = count // CHUNK
    total = 2 * lax.axis_size("blk")
    f32, i32, bf16 = jnp.float32, jnp.int32, jnp.bfloat16
    dma = pltpu.SemaphoreType.DMA
    vmem = pl.BlockSpec(memory_space=pltpu.VMEM)
    weight, mass = pl.pallas_call(
        kernel,
        out_shape=(jax.ShapeDtypeStruct((count,), f32), jax.ShapeDtypeStruct((CLUSTERS,), f32)),
        in_specs=[pl.BlockSpec(memory_space=pltpu.HBM)] * 2,
        out_specs=(vmem, vmem),
        scratch_shapes=[
            pltpu.VMEM((count, width), bf16),
            pltpu.VMEM((count,), i32),
            pltpu.VMEM((1, count), i32),
            pltpu.VMEM((total, 1, CLUSTERS), f32),
            pltpu.VMEM((count, width), bf16),
            pltpu.VMEM((count, width), bf16),
            pltpu.VMEM((count, width), bf16),
            pltpu.VMEM((count, width), bf16),
            pltpu.VMEM((2 * GROUP, 1, count), i32),
            pltpu.VMEM((5, count, 128), i32),
            pltpu.VMEM((count, 128), f32),
            pltpu.VMEM((1, count), f32),
            pltpu.VMEM((3, 1, count), f32),
            pltpu.VMEM((3, 1, count), f32),
            dma((n,)), dma((n,)), dma((n,)), dma((n,)), dma((2,)), dma((n,)), dma((n,)),
            dma((2 * GROUP - 1,)), dma((2 * GROUP,)), dma((3,)), dma((3,)),
            dma((2,)), dma((total,)), dma((total,)),
        ],
        compiler_params=pltpu.CompilerParams(
            collective_id=0, has_side_effects=True, vmem_limit_bytes=63 * 1024 * 1024),
        cost_estimate=pl.CostEstimate(flops=12 * count * count * width, bytes_accessed=2 * count * width,
                                      transcendentals=6 * count * count),
    )(embeddings, labels)
    return weight, mass


def solution(mesh):
    in_specs = (P(("parts", "blk", "sub"), None), P(("parts", "blk", "sub")))
    out_specs = (P(("parts", "blk", "sub")), P("parts"))
    return jax.shard_map(
        per_device, mesh=mesh, in_specs=in_specs, out_specs=out_specs, check_vma=False
    )
```

```python
import functools
import math

import jax
import jax.numpy as jnp
from jax import lax
from jax.experimental import pallas as pl
from jax.experimental.pallas import tpu as pltpu
from jax.sharding import PartitionSpec as P

CLUSTERS = 128
GROUP = 4
TAU = 25.0
MESH = pl.DeviceIdType.MESH
CHUNK = 256


def ring_swap(v):
    return v + lax.div(v, 2) - 2 * lax.div(v, 3)


def kernel(src, lab1, out_w, out_m, emb, flat, lab, masses, other, near, far, cross, labs, cols,
           near_sum, cross_sum, send_buf, back,
           near_send, near_recv, far_send, far_recv, other_sem, cross_send,
           cross_recv, lab_send, lab_recv, back_send, back_recv,
           local_sem, mass_send, mass_recv):
    count, width = emb.shape
    n = count // CHUNK
    scale = TAU * math.log2(math.e) / width
    part = lax.axis_index("parts")
    blk = lax.axis_index("blk")
    core = lax.axis_index("sub")
    low = lax.rem(blk, GROUP)
    base = blk - low
    place = ring_swap(low)
    step = 1 - 2 * core
    total = 2 * lax.axis_size("blk")
    index = 2 * blk + core
    load_lab = pltpu.make_async_copy(lab1, flat, local_sem.at[1])
    load_lab.start()

    def device(offset, c):
        return (part, base + ring_swap(lax.rem(place + offset + 2 * GROUP, GROUP)), c)

    me = place * 2 + core
    nxt = device(step, core)
    prv = device(-step, core)
    sib = device(0, 1 - core)
    opp = device(2, core)
    skew = device(step, 1 - core)

    def who(offset, c):
        return lax.rem(place + offset + 2 * GROUP, GROUP) * 2 + c

    others = [(o, x) for o in range(GROUP) for x in range(2) if (o, x) != (0, 0)]

    def member(k):
        t = lax.rem(index + k, total)
        return t, (part, lax.div(t, 2), lax.rem(t, 2))

    barrier = pltpu.get_barrier_semaphore()

    @pl.loop(1, total, unroll=5 if (total - 1) % 5 == 0 else 1)
    def _(k):
        pl.semaphore_signal(barrier, inc=1, device_id=member(k)[1], device_id_type=MESH)

    load = pltpu.make_async_copy(src, emb, local_sem.at[0])
    load.start()
    load_lab.wait()
    lab[...] = flat[...].reshape(1, count)
    pl.semaphore_wait(barrier, total - 1)

    def rows(c):
        return pl.ds(pl.multiple_of(c * CHUNK, CHUNK), CHUNK)

    def copy(src, dst, s, r, dev):
        return pltpu.make_async_remote_copy(src_ref=src, dst_ref=dst, send_sem=s, recv_sem=r,
                                            device_id=dev, device_id_type=MESH)

    def near_copy(c):
        return copy(src.at[rows(c)], near.at[rows(c)], near_send.at[c], near_recv.at[c], nxt)

    def far_copy(c):
        return copy(near.at[rows(c)], far.at[rows(c)], far_send.at[c], far_recv.at[c], nxt)

    def cross_copy(c):
        return copy(near.at[rows(c)], cross.at[rows(c)], cross_send.at[c], cross_recv.at[c], sib)

    def other_copy():
        return copy(src, other, other_sem.at[0], other_sem.at[1], sib)

    def lab_copy(k):
        o, x = others[k]
        c = x + core - 2 * x * core
        sent = copy(lab, labs.at[me], lab_send.at[k], lab_recv.at[me], device(o, c))
        src = who(o, c)
        got = copy(lab, labs.at[src], lab_send.at[k], lab_recv.at[src], device(o, c))
        return sent, got

    for k in range(len(others)):
        lab_copy(k)[0].start()

    @pl.loop(0, n)
    def _(c):
        near_copy(c).start()

    other_copy().start()

    def column(row):
        return jnp.broadcast_to(row, (128, count)).T

    own_lab = lab[...]
    cols[0] = column(own_lab)
    load.wait()

    def tile(x, xlab, y, ylab):
        s = lax.dot_general(x, y, (((1,), (1,)), ((), ())), preferred_element_type=jnp.float32)
        v = jnp.exp2((s - float(width)) * scale)
        same = jnp.concatenate([xlab] * (count // 128), axis=1) == ylab
        return jnp.where(same, v, 0.0)

    def colsum(v):
        return jnp.sum(v, axis=0, keepdims=True)

    def rowpart(v):
        t = v[:, :128]
        for k in range(1, count // 128):
            t = t + v[:, k * 128:(k + 1) * 128]
        return t

    def own_tile(ref, slot, c):
        return tile(ref[rows(c), :], cols[slot, rows(c), :], emb[...], own_lab)

    zero = jnp.zeros((1, count), jnp.float32)
    own = lax.fori_loop(0, n, lambda c, a: a + colsum(own_tile(emb, 0, c)), zero)

    for k in range(len(others)):
        sent, got = lab_copy(k)
        got.wait_recv()
    cols[1] = column(labs[who(0, 1 - core)])
    cols[2] = column(labs[who(-step, core)])
    cols[3] = column(labs[who(step, 1 - core)])
    cols[4] = column(labs[who(2, core)])
    cross_lab = labs[who(step, 1 - core)]

    def near_step(c, a):
        near_copy(c).wait_recv()
        far_copy(c).start()
        cross_copy(c).start()
        v = own_tile(near, 2, c)
        near_sum[rows(c), :] = rowpart(v)
        return a + colsum(v)

    own = lax.fori_loop(0, n, near_step, own)

    other_copy().wait_recv()
    own = lax.fori_loop(0, n, lambda c, a: a + colsum(own_tile(other, 1, c)), own)

    def cross_step(c, a):
        cross_copy(c).wait_recv()
        return a + colsum(own_tile(cross, 3, c))

    own = lax.fori_loop(0, n, cross_step, own)
    cross_sum[...] = zero

    @pl.when(core == 1)
    def _():
        @pl.loop(0, n)
        def _(c):
            v = tile(near[rows(c), :], cols[2, rows(c), :], cross[...], cross_lab)
            near_sum[rows(c), :] += rowpart(v)
            cross_sum[...] += colsum(v)

    def back_copy(k, dev):
        return copy(send_buf.at[k], back.at[k], back_send.at[k], back_recv.at[k], dev)

    send_buf[0] = colsum(near_sum[...].T)
    back_copy(0, prv).start()

    def far_step(c, a):
        far_copy(c).wait_recv()

        @pl.when(core == 0)
        def _():
            v = tile(far[rows(c), :], cols[4, rows(c), :], cross[...], cross_lab)
            send_buf[1, :, rows(c)] = colsum(rowpart(v).T)
            cross_sum[...] += colsum(v)

            @pl.when(c == n - 1)
            def _():
                send_buf[2] = cross_sum[...]
                back_copy(1, opp).start()
                back_copy(2, skew).start()

        @pl.when((core == 1) & (c == 0))
        def _():
            send_buf[1] = zero
            send_buf[2] = cross_sum[...]
            back_copy(1, opp).start()
            back_copy(2, skew).start()

        return a + colsum(own_tile(far, 4, c))

    own = lax.fori_loop(0, n, far_step, own)

    for k, dev in enumerate((prv, opp, skew)):
        back_copy(k, dev).wait_recv()
        own = own + back[k]

    weight = 1.0 / own
    ident = lax.broadcasted_iota(jnp.int32, (CLUSTERS, count), 0)
    masses[index] = colsum(rowpart(jnp.where(ident == own_lab, weight, 0.0)).T)

    def mass_copy(k):
        t, dev = member(k)
        sent = copy(masses.at[index], masses.at[index], mass_send.at[k], mass_recv.at[index], dev)
        got = copy(masses.at[t], masses.at[t], mass_send.at[k], mass_recv.at[t], dev)
        return sent, got

    @pl.loop(1, total, unroll=5 if (total - 1) % 5 == 0 else 1)
    def _(k):
        mass_copy(k)[0].start()

    out_w[...] = weight.reshape(count)

    @pl.loop(0, n)
    def _(c):
        near_copy(c).wait_send()
        far_copy(c).wait_send()
        cross_copy(c).wait_send()

    other_copy().wait_send()
    for k in range(len(others)):
        lab_copy(k)[0].wait_send()
    for k, dev in enumerate((prv, opp, skew)):
        back_copy(k, dev).wait_send()

    @pl.loop(1, total, unroll=5 if (total - 1) % 5 == 0 else 1)
    def _(k):
        mass_copy(k)[1].wait_recv()

    out_m[...] = jnp.sum(masses[...], axis=0).reshape(CLUSTERS)

    @pl.loop(1, total, unroll=5 if (total - 1) % 5 == 0 else 1)
    def _(k):
        mass_copy(k)[0].wait_send()


def per_device(embeddings, labels):
    count, width = embeddings.shape
    n = count // CHUNK
    total = 2 * lax.axis_size("blk")
    f32, i32, bf16 = jnp.float32, jnp.int32, jnp.bfloat16
    dma = pltpu.SemaphoreType.DMA
    vmem = pl.BlockSpec(memory_space=pltpu.VMEM)
    weight, mass = pl.pallas_call(
        kernel,
        out_shape=(jax.ShapeDtypeStruct((count,), f32), jax.ShapeDtypeStruct((CLUSTERS,), f32)),
        in_specs=[pl.BlockSpec(memory_space=pltpu.HBM)] * 2,
        out_specs=(vmem, vmem),
        scratch_shapes=[
            pltpu.VMEM((count, width), bf16),
            pltpu.VMEM((count,), i32),
            pltpu.VMEM((1, count), i32),
            pltpu.VMEM((total, 1, CLUSTERS), f32),
            pltpu.VMEM((count, width), bf16),
            pltpu.VMEM((count, width), bf16),
            pltpu.VMEM((count, width), bf16),
            pltpu.VMEM((count, width), bf16),
            pltpu.VMEM((2 * GROUP, 1, count), i32),
            pltpu.VMEM((5, count, 128), i32),
            pltpu.VMEM((count, 128), f32),
            pltpu.VMEM((1, count), f32),
            pltpu.VMEM((3, 1, count), f32),
            pltpu.VMEM((3, 1, count), f32),
            dma((n,)), dma((n,)), dma((n,)), dma((n,)), dma((2,)), dma((n,)), dma((n,)),
            dma((2 * GROUP - 1,)), dma((2 * GROUP,)), dma((3,)), dma((3,)),
            dma((2,)), dma((total,)), dma((total,)),
        ],
        compiler_params=pltpu.CompilerParams(
            collective_id=0, has_side_effects=True, vmem_limit_bytes=63 * 1024 * 1024),
        cost_estimate=pl.CostEstimate(flops=12 * count * count * width, bytes_accessed=2 * count * width,
                                      transcendentals=6 * count * count),
    )(embeddings, labels)
    return weight, mass


def solution(mesh):
    in_specs = (P(("parts", "blk", "sub"), None), P(("parts", "blk", "sub")))
    out_specs = (P(("parts", "blk", "sub")), P("parts"))
    return jax.shard_map(
        per_device, mesh=mesh, in_specs=in_specs, out_specs=out_specs, check_vma=False
    )
```
